32 devices in a mesh: parts: 2 (over x), bundle: 16 (over z, y, core).
Axes of the slice: x: 2, y: 2, z: 4, core: 2. Of those that a mesh axis runs over, the one named last changes fastest.
Arguments:
- dynamics: float32 [32, 512, 512], P(('parts', 'bundle')), parts along dimension 0, may hold values from -1 to 1
- inputs_map: float32 [32, 512, 512], P(('parts', 'bundle')), parts along dimension 0, may hold values from -1 to 1
- state_cost: float32 [512], replicated, may hold values from 0.5 to 2
- control_cost: float32 [512], replicated, may hold values from 0.5 to 2
- scenarios: int32 [32], P('parts'), parts along dimension 0, may hold values from 1 to 8
- node_ids: int32 [3, 32], P(None, 'parts'), parts along dimension 1, may hold values from 0 to 7, never falling along the last dimension, each value on 1 to 4 neighbouring positions
- multipliers: bfloat16 [3, 32, 512, 512], P(None, ('parts', 'bundle')), parts along dimension 1, may hold values from -0.25 to 0.25
- reference_gains: bfloat16 [3, 32, 512, 512], P(None, ('parts', 'bundle')), parts along dimension 1, may hold values from -0.25 to 0.25
Outputs:
- new_multipliers: bfloat16 [3, 32, 512, 512], P(None, ('parts', 'bundle')), parts along dimension 1
- average_gains: bfloat16 [3, 32, 512, 512], P(None, ('parts', 'bundle')), parts along dimension 1
The draws below stay inside these ranges and needn't reach their ends.
There are 2 independent parts, one for each index of `parts`. The reference program is written for one: setup_inputs(seed, part) draws one part's arguments, and reference() takes and returns one part's arrays. A program takes and returns all parts, laid end to end along the dimension named above; an argument that names none is the same for every part. Nothing has to cross between parts.
Inputs may be any that keep to these rules, and one draw needn't show every extreme that they name: `node_ids`: in every section the node ids never fall along the bundles; a node holds 1 to 4 consecutive bundles, one of them exactly 4.
All inputs are finite; a program needn't handle non-finite values.
Results may differ from the reference program's by a relative error of at most 0.0011.
Values sent between devices are 32-bit elements; how exact they have to be, the bound alone decides.
A program may use at most 192 MiB of HBM per device.

```python
import math
import jax
import jax.numpy as jnp
import numpy as np
from jax import lax

NS = 512
NU = 512
SECTIONS = 3
SPAN = 4
BUNDLES = 16


HIGH = lax.Precision.HIGHEST


def common_modes(key, strongest):
    mode_count = min(24, NS // 4)
    state_key, control_key, growth_key = jax.random.split(key, 3)
    half_width = math.sqrt(3.0)
    basis_state = jax.random.uniform(state_key, (NS, mode_count), jnp.float32, -half_width, half_width) / math.sqrt(NS)
    basis_control = jax.random.uniform(control_key, (NU, mode_count), jnp.float32, -half_width, half_width) / math.sqrt(NU)
    growth = jax.random.uniform(growth_key, (mode_count,), jnp.float32, 2.0, 4.0)
    ladder = jnp.arange(mode_count, dtype=jnp.float32) / (mode_count - 1)
    authority = 0.3 * jnp.exp(ladder * math.log(strongest / 0.3))
    return (basis_state, basis_control, growth, authority)


def draw_jitter(jitter_key, shape):
    return jnp.clip(jax.random.normal(jitter_key, shape, jnp.float32), -6.0, 6.0)


def draw_dynamics(key, part):
    strongest = 17.0
    basis_state, basis_control, growth, authority = common_modes(key, strongest)
    key = jax.random.fold_in(key, 11)
    jitter_key, spread_key = jax.random.split(key)
    jitter = draw_jitter(jitter_key, (BUNDLES, NS, NS)) / math.sqrt(4 * NS)
    factor = jax.random.uniform(spread_key, (BUNDLES, 1), jnp.float32, 0.85, 1.15)
    strengths = factor * growth[None, :]
    low_rank = jnp.einsum('im,bm,jm->bij', basis_state, strengths, basis_state, precision=HIGH)
    return jnp.clip(jitter + low_rank, -1.0, 1.0)


def draw_inputs_map(key, part):
    strongest = 17.0
    basis_state, basis_control, growth, authority = common_modes(key, strongest)
    key = jax.random.fold_in(key, 23)
    jitter_key, spread_key = jax.random.split(key)
    jitter = draw_jitter(jitter_key, (BUNDLES, NS, NU)) / math.sqrt(4 * NU)
    factor = jax.random.uniform(spread_key, (BUNDLES, 1), jnp.float32, 0.85, 1.15)
    strengths = factor * authority[None, :]
    low_rank = jnp.einsum('im,bm,jm->bij', basis_state, strengths, basis_control, precision=HIGH)
    return jnp.clip(jitter + low_rank, -1.0, 1.0)


def place_ends(drawn, stream_key, least, top_value):
    dims = drawn.shape
    spot = [jax.random.randint(jax.random.fold_in(stream_key, axis), (), 0, dims[axis]) for axis in range(len(dims))]
    drawn = drawn.at[tuple(spot)].set(least)
    longest = dims.index(max(dims))
    spot[longest] = (spot[longest] + 1) % dims[longest]
    return drawn.at[tuple(spot)].set(top_value)


def block_levels(own_key, shape, cuts, smallest, largest):
    def one(position, parts):
        draws = jax.random.uniform(jax.random.fold_in(jax.random.fold_in(own_key, 6), position), (parts,), jnp.float32, smallest / len(cuts), largest / len(cuts))
        return jnp.repeat(jnp.exp(draws), shape[position] // parts).reshape((-1,) + (1,) * (len(shape) - position - 1))

    level = one(*cuts[0])
    for cut in cuts[1:]:
        level = level * one(*cut)
    return level


def profile(amount, total, bound, lean):
    loads = [(1 << 20) // math.isqrt(standing ** lean) + 1 for standing in range(2, amount + 1)]
    surplus, counts = total - bound - (amount - 1), [1] * (amount - 1)
    while surplus > 0:
        free = [i for i in range(amount - 1) if counts[i] < bound]
        mass, left = sum([loads[i] for i in free]), surplus
        for i in free:
            more = min(bound - counts[i], max(1, left * loads[i] // mass), surplus)
            counts[i] = counts[i] + more
            surplus = surplus - more
    return np.array([bound] + counts)


def ragged(rng, number_of, total, most, skew):
    if number_of == 2:
        one = jax.random.randint(rng, (), max(1, total - most), min(most, total - 1) + 1)
        return jnp.stack([one, total - one])
    tallies = jnp.asarray(profile(number_of, total, most, skew), jnp.int32)
    pairs = (number_of - 1) // 2
    giver, receiver = tallies[1:1 + 2 * pairs:2], tallies[2:2 + 2 * pairs:2]
    slack = jnp.minimum(giver - 1, most - receiver)
    shifted = jax.random.randint(jax.random.fold_in(rng, 1), (pairs,), 0, 1 << 20) % (slack + 1)
    tallies = tallies.at[1:1 + 2 * pairs:2].set(giver - shifted).at[2:2 + 2 * pairs:2].set(receiver + shifted)
    return tallies[jax.random.permutation(jax.random.fold_in(rng, 2), number_of)]


def centred(key, shape, spread, most, shards=(), held_as=jnp.bfloat16):
    array = spread * jax.random.normal(key, shape, jnp.float32)
    if shards:
        array = array * block_levels(key, shape, shards, -0.22, 0.18)
    return jnp.clip(array, -most, most).astype(held_as)


def setup_inputs(seed: int = 0, part: int = 0) -> dict:
    seeds = jax.random.split(jax.random.key(seed), 9)
    own_keys = jax.random.split(jax.random.fold_in(seeds[8], part), 9)
    dynamics = draw_dynamics(jax.random.fold_in(jax.random.fold_in(seeds[8], part), 71), part)
    inputs_map = draw_inputs_map(jax.random.fold_in(jax.random.fold_in(seeds[8], part), 71), part)
    state_cost = jnp.clip(jnp.exp(jax.random.uniform(seeds[2], (NS,), jnp.float32, math.log(0.5), math.log(2.0))), 0.5, 2.0)
    control_cost = jnp.clip(jnp.exp(jax.random.uniform(seeds[3], (NU,), jnp.float32, math.log(0.5), math.log(2.0))), 0.5, 2.0)
    scenarios = place_ends(jax.random.randint(own_keys[4], (BUNDLES,), 1, 9), jax.random.fold_in(own_keys[4], 1), 1, 8).astype(jnp.int32)
    node_ids = jax.vmap(lambda own: jnp.searchsorted(jnp.cumsum(ragged(own, BUNDLES // 2, BUNDLES, SPAN, 1)), jnp.arange(BUNDLES), side="right"))(jax.random.split(own_keys[5], SECTIONS)).reshape((SECTIONS, BUNDLES)).astype(jnp.int32)
    multipliers = centred(own_keys[6], (SECTIONS, BUNDLES, NU, NS), NS ** -0.5, 0.25, ((1, 16),))
    reference_gains = centred(own_keys[7], (SECTIONS, BUNDLES, NU, NS), NS ** -0.5, 0.25, ((1, 16),))
    return dict(dynamics=dynamics, inputs_map=inputs_map, state_cost=state_cost, control_cost=control_cost, scenarios=scenarios, node_ids=node_ids, multipliers=multipliers, reference_gains=reference_gains)


RHO = 1.0
HIGH = lax.Precision.HIGHEST

def bundle_gain(cost_now, A, B, r_diag, lam, kref):
    BP = jnp.dot(B.T, cost_now, precision=HIGH)
    H = jnp.dot(BP, B, precision=HIGH) + jnp.diag(r_diag + RHO)
    G = jnp.dot(BP, A, precision=HIGH)
    factor = jnp.linalg.cholesky(H)
    gain = jax.scipy.linalg.cho_solve((factor, True), G - lam + RHO * kref)
    return (H, G, gain)

def next_cost(cost_now, A, H, G, kbar, q_diag):
    apa = jnp.dot(A.T, jnp.dot(cost_now, A, precision=HIGH), precision=HIGH)
    cross = jnp.dot(G.T, kbar, precision=HIGH)
    quad = jnp.dot(kbar.T, jnp.dot(H, kbar, precision=HIGH), precision=HIGH)
    return jnp.diag(q_diag) + apa - cross - cross.T + quad

def reference(dynamics, inputs_map, state_cost, control_cost, scenarios, node_ids, multipliers, reference_gains):
    weights = scenarios.astype(jnp.float32)
    cost_now = jnp.broadcast_to(jnp.diag(state_cost), (BUNDLES, NS, NS))
    lam_list = [None] * SECTIONS
    avg_list = [None] * SECTIONS
    for section in reversed(range(SECTIONS)):
        lam = multipliers[section].astype(jnp.float32)
        kref = reference_gains[section].astype(jnp.float32)
        H, G, gain = jax.vmap(bundle_gain, in_axes=(0, 0, 0, None, 0, 0))(cost_now, dynamics, inputs_map, control_cost, lam, kref)
        row = node_ids[section]
        same = (row[:, None] == row[None, :]).astype(jnp.float32) * weights[None, :]
        total = jnp.sum(same, axis=1)
        summed = jnp.einsum('bc,cij->bij', same, gain, precision=HIGH)
        kbar = summed / total[:, None, None]
        lam_list[section] = (lam + RHO * (gain - kbar)).astype(jnp.bfloat16)
        avg_list[section] = kbar.astype(jnp.bfloat16)
        cost_now = jax.vmap(next_cost, in_axes=(0, 0, 0, 0, 0, None))(cost_now, dynamics, H, G, kbar, state_cost)
    return (jnp.stack(lam_list), jnp.stack(avg_list))
```

```python
import functools

import jax
import jax.numpy as jnp
from jax import lax
from jax.experimental import pallas as pl
from jax.experimental.pallas import tpu as pltpu
from jax.sharding import PartitionSpec as P

RHO = 1.0
SPAN = 4
BLOCK = 128
PIVOTS = 4
CHUNKS = 4
F32 = jnp.float32
BF16 = jnp.bfloat16


def split(x):
    high = x.astype(BF16)
    return high, (x - high.astype(F32)).astype(BF16)


def dot3(a, b):
    a_high, a_low = split(a)
    b_high, b_low = split(b)
    d = functools.partial(jnp.dot, preferred_element_type=F32)
    return d(a_high, b_high) + (d(a_high, b_low) + d(a_low, b_high))


def dot6(a, b):
    return jnp.dot(a, b, precision=lax.Precision.HIGHEST, preferred_element_type=F32)


def tile(index, size):
    return pl.ds(pl.multiple_of(index * size, size), size)


def negative_inverse(block):
    n = block.shape[0]
    slabs = [block[s : s + 8, :] for s in range(0, n, 8)]
    shape = (8, n)
    lane = lax.broadcasted_iota(jnp.int32, shape, 1)
    sub = lax.broadcasted_iota(jnp.int32, shape, 0)
    g = PIVOTS
    for k in range(0, n, g):
        p, o = k // 8, k % 8
        cols = [
            [jnp.broadcast_to(slab[:, k + i : k + i + 1], shape) for slab in slabs]
            for i in range(g)
        ]
        rows = [jnp.broadcast_to(slabs[p][o + i : o + i + 1, :], shape) for i in range(g)]
        e = {}
        for i in range(g):
            for j in range(i + 1):
                e[i, j] = jnp.broadcast_to(cols[j][p][o + i : o + i + 1, :], shape)
        for q in range(g):
            d = 1.0 / e[q, q]
            col = [e[max(i, q), min(i, q)] for i in range(g)]
            scaled = [c * d for c in col]
            for i in range(g):
                for j in range(i + 1):
                    if i != q and j != q:
                        e[i, j] = e[i, j] - scaled[i] * col[j]
            for i in range(g):
                e[max(i, q), min(i, q)] = -d if i == q else scaled[i]
        hats = []
        for i in range(g):
            ei = [e[max(i, j), min(i, j)] for j in range(g)]
            hat = -(ei[0] * rows[0])
            for j in range(1, g):
                hat = hat - ei[j] * rows[j]
            for j in range(g):
                hat = jnp.where(lane == k + j, ei[j], hat)
            hats.append(hat)
        inside = (lane >= k) & (lane < k + g)
        updated = []
        for s, slab in enumerate(slabs):
            new = jnp.where(inside, 0.0, slab)
            for i in range(g):
                new = new - cols[i][s] * hats[i]
            if s == p:
                for i in range(g):
                    new = jnp.where(sub == o + i, hats[i], new)
            updated.append(new)
        slabs = updated
    return jnp.concatenate(slabs, axis=0)


def kernel(
    count,
    ids,
    scen,
    a_ref,
    b_ref,
    q_ref,
    r_ref,
    lam_ref,
    kref_ref,
    lam_out,
    avg_out,
    at,
    bt,
    cost,
    pa,
    pb,
    h,
    m,
    g,
    w,
    gain,
    own,
    part,
    kbar,
    kt,
    par,
    near,
    far,
    cross,
    send_sem,
    recv_sem,
):
    sections = lam_ref.shape[0]
    n = a_ref.shape[-1]
    rows = n // CHUNKS
    place = lax.axis_index("bundle")
    step = 2 * lax.rem(place, 2) - 1
    partner = place - step

    def inside(target):
        return (target >= 0) & (target < count)

    near_at, far_at, cross_at = place + step, place + 3 * step, place - 2 * step
    has_near, has_far, has_cross = inside(near_at), inside(far_at), inside(cross_at)

    barrier = pltpu.get_barrier_semaphore()

    def greet(target):
        pl.semaphore_signal(
            barrier, inc=1, device_id={"bundle": target}, device_id_type=pl.DeviceIdType.MESH
        )

    greet(partner)

    @pl.when(has_near)
    def _():
        greet(near_at)

    @pl.when(has_far)
    def _():
        greet(far_at)

    def both(f, tiles, size):
        lax.fori_loop(0, tiles, lambda i, c: (f(tile(i, size)), c)[1], 0)

    def transpose(out, load):
        def one(t):
            out[:, t] = load(t).T

        both(one, n // BLOCK, BLOCK)

    transpose(at, lambda t: a_ref[0, t, :])
    transpose(bt, lambda t: b_ref[0, t, :])

    def diagonal(t_index, row, size):
        i = lax.broadcasted_iota(jnp.int32, (size, n), 0) + t_index * size
        j = lax.broadcasted_iota(jnp.int32, (size, n), 1)
        return jnp.where(i == j, row, 0.0)

    def start(i, c):
        cost[tile(i, BLOCK), :] = diagonal(i, q_ref[...], BLOCK)
        return c

    lax.fori_loop(0, n // BLOCK, start, 0)

    pl.semaphore_wait(barrier, 1 + has_near.astype(jnp.int32) + has_far.astype(jnp.int32))

    half = n // 2

    def section_step(turn, carry):
        section = sections - 1 - turn

        def id_at(target):
            return ids[section, jnp.clip(target, 0, count - 1)]

        mine = id_at(place)

        def same(target):
            return inside(target) & (id_at(target) == mine)

        total = jnp.int32(0)
        for reach in range(1 - SPAN, SPAN):
            target = place + reach
            weight = scen[jnp.clip(target, 0, count - 1)]
            total = total + jnp.where(same(target), weight, 0)
        total = total.astype(F32)
        own_weight = scen[place].astype(F32)

        def products(t):
            pa[:, t] = dot3(cost[...], a_ref[0, :, t])
            pb[:, t] = dot3(cost[...], b_ref[0, :, t])

        both(products, 2, half)

        def more(t):
            h[:, t] = dot3(bt[...], pb[:, t])
            g[:, t] = dot3(bt[...], pa[:, t])

        both(more, 2, half)

        def finish(i, c):
            t = tile(i, BLOCK)
            full = h[t, :] + diagonal(i, r_ref[...] + RHO, BLOCK)
            h[t, :] = full
            m[t, :] = full
            w[t, :] = (
                g[t, :]
                - lam_ref[section, 0, t, :].astype(F32)
                + RHO * kref_ref[section, 0, t, :].astype(F32)
            )
            return c

        lax.fori_loop(0, n // BLOCK, finish, 0)

        def sweep(i, c):
            t = tile(i, BLOCK)
            minus = negative_inverse(m[t, t])
            row_hat = -dot6(minus, m[t, :])
            col = m[:, t]
            col_hat = -dot6(col, minus)
            m[...] = m[...] - dot6(col, row_hat)
            m[t, :] = row_hat
            m[:, t] = col_hat
            m[t, t] = minus
            return c

        lax.fori_loop(0, n // BLOCK, sweep, 0)

        def copy(src, dst, kind, r, target):
            return pltpu.make_async_remote_copy(
                src_ref=src,
                dst_ref=dst,
                send_sem=send_sem.at[section, kind, r],
                recv_sem=recv_sem.at[section, kind, r],
                device_id={"bundle": target},
                device_id_type=pl.DeviceIdType.MESH,
            )

        def to_partner(r):
            t = tile(r, rows)
            return copy(own.at[t, :], par.at[section, t, :], 0, r, partner)

        def to_near(r):
            t = tile(r, rows)
            return copy(part.at[t, :], near.at[section, t, :], 1, r, near_at)

        def to_far(r):
            t = tile(r, rows)
            return copy(part.at[t, :], far.at[section, t, :], 2, r, far_at)

        def to_cross(r):
            t = tile(r, rows)
            return copy(near.at[section, t, :], cross.at[section, t, :], 3, r, partner)

        def solve(r, c):
            t = tile(r, rows)
            value = -dot3(m[t, :], w[...])
            gain[t, :] = value
            own[t, :] = own_weight * value
            to_partner(r).start()
            return c

        lax.fori_loop(0, CHUNKS, solve, 0)

        def pair(r, c):
            t = tile(r, rows)
            to_partner(r).wait_recv()
            part[t, :] = own[t, :] + jnp.where(same(partner), par[section, t, :], 0.0)

            @pl.when(has_near)
            def _():
                to_near(r).start()

            @pl.when(has_far)
            def _():
                to_far(r).start()

            return c

        lax.fori_loop(0, CHUNKS, pair, 0)

        def onward(r, c):
            @pl.when(has_near)
            def _():
                to_near(r).wait_recv()
                to_cross(r).start()

            return c

        lax.fori_loop(0, CHUNKS, onward, 0)

        def gather(r, c):
            t = tile(r, rows)
            kbar[t, :] = part[t, :]

            @pl.when(has_near)
            def _():
                kbar[t, :] = kbar[t, :] + jnp.where(same(near_at), near[section, t, :], 0.0)

            @pl.when(has_far)
            def _():
                to_far(r).wait_recv()
                kbar[t, :] = kbar[t, :] + jnp.where(same(far_at), far[section, t, :], 0.0)

            @pl.when(has_cross)
            def _():
                to_cross(r).wait_recv()
                kbar[t, :] = kbar[t, :] + jnp.where(same(cross_at), cross[section, t, :], 0.0)

            average = kbar[t, :] / jnp.full((rows, n), total)
            kbar[t, :] = average
            kt[:, t] = average.T
            avg_out[section, 0, t, :] = average.astype(BF16)
            lam_out[section, 0, t, :] = (
                lam_ref[section, 0, t, :].astype(F32) + RHO * (gain[t, :] - average)
            ).astype(BF16)
            return c

        lax.fori_loop(0, CHUNKS, gather, 0)

        def sent(r, c):
            to_partner(r).wait_send()

            @pl.when(has_near)
            def _():
                to_near(r).wait_send()
                to_cross(r).wait_send()

            @pl.when(has_far)
            def _():
                to_far(r).wait_send()

            return c

        lax.fori_loop(0, CHUNKS, sent, 0)

        @pl.when(section > 0)
        def _():
            def gt(i, c):
                t = tile(i, BLOCK)
                m[:, t] = g[t, :].T
                return c

            lax.fori_loop(0, n // BLOCK, gt, 0)

            def residual(t):
                w[:, t] = dot3(h[...], kbar[:, t]) - g[:, t]

            both(residual, 2, half)

            def base(t):
                cost[:, t] = dot3(at[...], pa[:, t]) - dot3(m[...], kbar[:, t])

            both(base, 2, half)

            def quad(t):
                cost[:, t] = cost[:, t] + dot3(kt[...], w[:, t])

            both(quad, 2, half)

            def diag(i, c):
                t = tile(i, BLOCK)
                cost[t, :] = cost[t, :] + diagonal(i, q_ref[...], BLOCK)
                return c

            lax.fori_loop(0, n // BLOCK, diag, 0)

        return carry

    lax.fori_loop(0, sections, section_step, 0)


def per_device(A, B, q, r, scenarios, node_ids, multipliers, reference_gains):
    sections = multipliers.shape[0]
    n = A.shape[-1]
    count = lax.axis_size("bundle")
    vmem = pl.BlockSpec(memory_space=pltpu.VMEM)
    smem = pl.BlockSpec(memory_space=pltpu.SMEM)
    square = pltpu.VMEM((n, n), F32)
    stack = pltpu.VMEM((sections, n, n), F32)
    out = jax.ShapeDtypeStruct(multipliers.shape, BF16)
    return pl.pallas_call(
        functools.partial(kernel, count),
        out_shape=(out, out),
        in_specs=[smem, smem] + [vmem] * 6,
        out_specs=(vmem, vmem),
        scratch_shapes=[square] * 14
        + [stack] * 4
        + [
            pltpu.SemaphoreType.DMA((sections, 4, CHUNKS)),
            pltpu.SemaphoreType.DMA((sections, 4, CHUNKS)),
        ],
        compiler_params=pltpu.CompilerParams(
            collective_id=0, has_side_effects=True, vmem_limit_bytes=56 * 1024 * 1024
        ),
    )(
        node_ids,
        scenarios,
        A,
        B,
        q.reshape(1, n),
        r.reshape(1, n),
        multipliers,
        reference_gains,
    )


def solution(mesh):
    placed = (
        P(("parts", "bundle"), None, None),
        P(("parts", "bundle"), None, None),
        P(),
        P(),
        P("parts"),
        P(None, "parts"),
        P(None, ("parts", "bundle"), None, None),
        P(None, ("parts", "bundle"), None, None),
    )
    return jax.shard_map(
        per_device,
        mesh=mesh,
        in_specs=placed,
        out_specs=(
            P(None, ("parts", "bundle"), None, None),
            P(None, ("parts", "bundle"), None, None),
        ),
        check_vma=False,
    )
```

```python
import functools

import jax
import jax.numpy as jnp
from jax import lax
from jax.experimental import pallas as pl
from jax.experimental.pallas import tpu as pltpu
from jax.sharding import PartitionSpec as P

RHO = 1.0
SPAN = 4
BLOCK = 128
PIVOTS = 8
CHUNKS = 4
F32 = jnp.float32
BF16 = jnp.bfloat16


def split(x):
    high = x.astype(BF16)
    return high, (x - high.astype(F32)).astype(BF16)


def dot3(a, b):
    a_high, a_low = split(a)
    b_high, b_low = split(b)
    d = functools.partial(jnp.dot, preferred_element_type=F32)
    return d(a_high, b_high) + (d(a_high, b_low) + d(a_low, b_high))


def dot6(a, b):
    return jnp.dot(a, b, precision=lax.Precision.HIGHEST, preferred_element_type=F32)


def tile(index, size):
    return pl.ds(pl.multiple_of(index * size, size), size)


def negative_inverse(block):
    n = block.shape[0]
    slabs = [block[s : s + 8, :] for s in range(0, n, 8)]
    shape = (8, n)
    lane = lax.broadcasted_iota(jnp.int32, shape, 1)
    sub = lax.broadcasted_iota(jnp.int32, shape, 0)
    g = PIVOTS
    for k in range(0, n, g):
        p, o = k // 8, k % 8
        cols = [
            [jnp.broadcast_to(slab[:, k + i : k + i + 1], shape) for slab in slabs]
            for i in range(g)
        ]
        rows = [jnp.broadcast_to(slabs[p][o + i : o + i + 1, :], shape) for i in range(g)]
        e = {}
        for i in range(g):
            for j in range(i + 1):
                e[i, j] = jnp.broadcast_to(cols[j][p][o + i : o + i + 1, :], shape)
        for q in range(g):
            d = 1.0 / e[q, q]
            col = [e[max(i, q), min(i, q)] for i in range(g)]
            scaled = [c * d for c in col]
            for i in range(g):
                for j in range(i + 1):
                    if i != q and j != q:
                        e[i, j] = e[i, j] - scaled[i] * col[j]
            for i in range(g):
                e[max(i, q), min(i, q)] = -d if i == q else scaled[i]
        hats = []
        for i in range(g):
            ei = [e[max(i, j), min(i, j)] for j in range(g)]
            hat = -(ei[0] * rows[0])
            for j in range(1, g):
                hat = hat - ei[j] * rows[j]
            for j in range(g):
                hat = jnp.where(lane == k + j, ei[j], hat)
            hats.append(hat)
        inside = (lane >= k) & (lane < k + g)
        updated = []
        for s, slab in enumerate(slabs):
            new = jnp.where(inside, 0.0, slab)
            for i in range(g):
                new = new - cols[i][s] * hats[i]
            if s == p:
                for i in range(g):
                    new = jnp.where(sub == o + i, hats[i], new)
            updated.append(new)
        slabs = updated
    return jnp.concatenate(slabs, axis=0)


def kernel(
    count,
    ids,
    scen,
    a_ref,
    b_ref,
    q_ref,
    r_ref,
    lam_ref,
    kref_ref,
    lam_out,
    avg_out,
    at,
    bt,
    cost,
    pa,
    pb,
    h,
    m,
    g,
    w,
    gain,
    own,
    part,
    kbar,
    kt,
    par,
    near,
    far,
    cross,
    send_sem,
    recv_sem,
):
    sections = lam_ref.shape[0]
    n = a_ref.shape[-1]
    rows = n // CHUNKS
    place = lax.axis_index("bundle")
    step = 2 * lax.rem(place, 2) - 1
    partner = place - step

    def inside(target):
        return (target >= 0) & (target < count)

    near_at, far_at, cross_at = place + step, place + 3 * step, place - 2 * step
    has_near, has_far, has_cross = inside(near_at), inside(far_at), inside(cross_at)

    barrier = pltpu.get_barrier_semaphore()

    def greet(target):
        pl.semaphore_signal(
            barrier, inc=1, device_id={"bundle": target}, device_id_type=pl.DeviceIdType.MESH
        )

    greet(partner)

    @pl.when(has_near)
    def _():
        greet(near_at)

    @pl.when(has_far)
    def _():
        greet(far_at)

    def both(f, tiles, size):
        lax.fori_loop(0, tiles, lambda i, c: (f(tile(i, size)), c)[1], 0)

    def transpose(out, load):
        def one(t):
            out[:, t] = load(t).T

        both(one, n // BLOCK, BLOCK)

    transpose(at, lambda t: a_ref[0, t, :])
    transpose(bt, lambda t: b_ref[0, t, :])

    def diagonal(t_index, row, size):
        i = lax.broadcasted_iota(jnp.int32, (size, n), 0) + t_index * size
        j = lax.broadcasted_iota(jnp.int32, (size, n), 1)
        return jnp.where(i == j, row, 0.0)

    def start(i, c):
        cost[tile(i, BLOCK), :] = diagonal(i, q_ref[...], BLOCK)
        return c

    lax.fori_loop(0, n // BLOCK, start, 0)

    pl.semaphore_wait(barrier, 1 + has_near.astype(jnp.int32) + has_far.astype(jnp.int32))

    half = n // 2

    def section_step(turn, carry):
        section = sections - 1 - turn

        def id_at(target):
            return ids[section, jnp.clip(target, 0, count - 1)]

        mine = id_at(place)

        def same(target):
            return inside(target) & (id_at(target) == mine)

        total = jnp.int32(0)
        for reach in range(1 - SPAN, SPAN):
            target = place + reach
            weight = scen[jnp.clip(target, 0, count - 1)]
            total = total + jnp.where(same(target), weight, 0)
        total = total.astype(F32)
        own_weight = scen[place].astype(F32)

        def products(t):
            pa[:, t] = dot3(cost[...], a_ref[0, :, t])
            pb[:, t] = dot3(cost[...], b_ref[0, :, t])

        both(products, 2, half)

        def more(t):
            h[:, t] = dot3(bt[...], pb[:, t])
            g[:, t] = dot3(bt[...], pa[:, t])

        both(more, 2, half)

        def finish(i, c):
            t = tile(i, BLOCK)
            full = h[t, :] + diagonal(i, r_ref[...] + RHO, BLOCK)
            h[t, :] = full
            m[t, :] = full
            w[t, :] = (
                g[t, :]
                - lam_ref[section, 0, t, :].astype(F32)
                + RHO * kref_ref[section, 0, t, :].astype(F32)
            )
            return c

        lax.fori_loop(0, n // BLOCK, finish, 0)

        def sweep(i, c):
            t = tile(i, BLOCK)
            minus = negative_inverse(m[t, t])
            row_hat = -dot6(minus, m[t, :])
            col = m[:, t]
            col_hat = -dot6(col, minus)
            m[...] = m[...] - dot6(col, row_hat)
            m[t, :] = row_hat
            m[:, t] = col_hat
            m[t, t] = minus
            return c

        lax.fori_loop(0, n // BLOCK, sweep, 0)

        def copy(src, dst, kind, r, target):
            return pltpu.make_async_remote_copy(
                src_ref=src,
                dst_ref=dst,
                send_sem=send_sem.at[section, kind, r],
                recv_sem=recv_sem.at[section, kind, r],
                device_id={"bundle": target},
                device_id_type=pl.DeviceIdType.MESH,
            )

        def to_partner(r):
            t = tile(r, rows)
            return copy(own.at[t, :], par.at[section, t, :], 0, r, partner)

        def to_near(r):
            t = tile(r, rows)
            return copy(part.at[t, :], near.at[section, t, :], 1, r, near_at)

        def to_far(r):
            t = tile(r, rows)
            return copy(part.at[t, :], far.at[section, t, :], 2, r, far_at)

        def to_cross(r):
            t = tile(r, rows)
            return copy(near.at[section, t, :], cross.at[section, t, :], 3, r, partner)

        def solve(r, c):
            t = tile(r, rows)
            value = -dot3(m[t, :], w[...])
            gain[t, :] = value
            own[t, :] = own_weight * value
            to_partner(r).start()
            return c

        lax.fori_loop(0, CHUNKS, solve, 0)

        def pair(r, c):
            t = tile(r, rows)
            to_partner(r).wait_recv()
            part[t, :] = own[t, :] + jnp.where(same(partner), par[section, t, :], 0.0)

            @pl.when(has_near)
            def _():
                to_near(r).start()

            @pl.when(has_far)
            def _():
                to_far(r).start()

            return c

        lax.fori_loop(0, CHUNKS, pair, 0)

        def onward(r, c):
            @pl.when(has_near)
            def _():
                to_near(r).wait_recv()
                to_cross(r).start()

            return c

        lax.fori_loop(0, CHUNKS, onward, 0)

        def gather(r, c):
            t = tile(r, rows)
            kbar[t, :] = part[t, :]

            @pl.when(has_near)
            def _():
                kbar[t, :] = kbar[t, :] + jnp.where(same(near_at), near[section, t, :], 0.0)

            @pl.when(has_far)
            def _():
                to_far(r).wait_recv()
                kbar[t, :] = kbar[t, :] + jnp.where(same(far_at), far[section, t, :], 0.0)

            @pl.when(has_cross)
            def _():
                to_cross(r).wait_recv()
                kbar[t, :] = kbar[t, :] + jnp.where(same(cross_at), cross[section, t, :], 0.0)

            average = kbar[t, :] / jnp.full((rows, n), total)
            kbar[t, :] = average
            kt[:, t] = average.T
            avg_out[section, 0, t, :] = average.astype(BF16)
            lam_out[section, 0, t, :] = (
                lam_ref[section, 0, t, :].astype(F32) + RHO * (gain[t, :] - average)
            ).astype(BF16)
            return c

        lax.fori_loop(0, CHUNKS, gather, 0)

        def sent(r, c):
            to_partner(r).wait_send()

            @pl.when(has_near)
            def _():
                to_near(r).wait_send()
                to_cross(r).wait_send()

            @pl.when(has_far)
            def _():
                to_far(r).wait_send()

            return c

        lax.fori_loop(0, CHUNKS, sent, 0)

        @pl.when(section > 0)
        def _():
            def gt(i, c):
                t = tile(i, BLOCK)
                m[:, t] = g[t, :].T
                return c

            lax.fori_loop(0, n // BLOCK, gt, 0)

            def residual(t):
                w[:, t] = dot3(h[...], kbar[:, t]) - g[:, t]

            both(residual, 2, half)

            def base(t):
                cost[:, t] = dot3(at[...], pa[:, t]) - dot3(m[...], kbar[:, t])

            both(base, 2, half)

            def quad(t):
                cost[:, t] = cost[:, t] + dot3(kt[...], w[:, t])

            both(quad, 2, half)

            def diag(i, c):
                t = tile(i, BLOCK)
                cost[t, :] = cost[t, :] + diagonal(i, q_ref[...], BLOCK)
                return c

            lax.fori_loop(0, n // BLOCK, diag, 0)

        return carry

    lax.fori_loop(0, sections, section_step, 0)


def per_device(A, B, q, r, scenarios, node_ids, multipliers, reference_gains):
    sections = multipliers.shape[0]
    n = A.shape[-1]
    count = lax.axis_size("bundle")
    vmem = pl.BlockSpec(memory_space=pltpu.VMEM)
    smem = pl.BlockSpec(memory_space=pltpu.SMEM)
    square = pltpu.VMEM((n, n), F32)
    stack = pltpu.VMEM((sections, n, n), F32)
    out = jax.ShapeDtypeStruct(multipliers.shape, BF16)
    return pl.pallas_call(
        functools.partial(kernel, count),
        out_shape=(out, out),
        in_specs=[smem, smem] + [vmem] * 6,
        out_specs=(vmem, vmem),
        scratch_shapes=[square] * 14
        + [stack] * 4
        + [
            pltpu.SemaphoreType.DMA((sections, 4, CHUNKS)),
            pltpu.SemaphoreType.DMA((sections, 4, CHUNKS)),
        ],
        compiler_params=pltpu.CompilerParams(
            collective_id=0, has_side_effects=True, vmem_limit_bytes=56 * 1024 * 1024
        ),
    )(
        node_ids,
        scenarios,
        A,
        B,
        q.reshape(1, n),
        r.reshape(1, n),
        multipliers,
        reference_gains,
    )


def solution(mesh):
    placed = (
        P(("parts", "bundle"), None, None),
        P(("parts", "bundle"), None, None),
        P(),
        P(),
        P("parts"),
        P(None, "parts"),
        P(None, ("parts", "bundle"), None, None),
        P(None, ("parts", "bundle"), None, None),
    )
    return jax.shard_map(
        per_device,
        mesh=mesh,
        in_specs=placed,
        out_specs=(
            P(None, ("parts", "bundle"), None, None),
            P(None, ("parts", "bundle"), None, None),
        ),
        check_vma=False,
    )
```
